32 devices in a mesh: role: 4 (over y, core), rep: 2 (over x), tp: 4 (over z).
Axes of the slice: x: 2, y: 2, z: 4, core: 2. Of those that a mesh axis runs over, the one named last changes fastest.
Arguments:
- span_hidden: bfloat16 [4096, 8192], P(('role', 'rep'), 'tp'), may hold values from -6 to 6
- key_value_weight: bfloat16 [8192, 2048], P('tp'), may hold values from -0.0625 to 0.0625
- queries: bfloat16 [128, 8192], P(('role', 'rep'), 'tp'), may hold values from -200 to 200
- kv_cache: bfloat16 [36864, 2048], P(('role', 'rep'), 'tp'), may hold values from -6 to 6, as said below
- block_table: int32 [128, 4], P(('role', 'rep')), may hold values from 0 to 35, as said below
- lengths: int32 [128], P(('role', 'rep')), may hold values from 1 to 512, as said below
- placement: int32 [8], replicated, may hold values from 0 to 127
Outputs:
- attention_out: bfloat16 [128, 8192], P(('role', 'rep'), 'tp')
The draws below stay inside these ranges and needn't reach their ends.
Inputs may be any that keep to these rules, and one draw needn't show every extreme that they name: `lengths`: one request of every replica has exactly 512 cached tokens. `block_table`: the first ceil(lengths / 128) entries of a request's row are distinct pages used by no other request of its replica; later entries are arbitrary pages of the pool. `kv_cache`: the 1 column blocks that hold the same KV head are equal.
All inputs are finite; a program needn't handle non-finite values.
Results may differ from the reference program's by a relative error of at most 0.0045.
Values may be sent and summed in bfloat16 or wider, within the bound.
A program may use at most 128 MiB of HBM per device.

```python
import jax
import jax.numpy as jnp
import numpy as np
from jax import lax

MODEL_WIDTH = 8192
QUERY_HEADS = 64
KEY_VALUE_HEADS = 8
HEAD_SIZE = 128
PAGE_TOKENS = 128
MAXP = 4
PREFILL_TOKENS = 512
DECODE_REQUESTS = 16
INSTANCE_COUNT = 8
REPLICA_PAGES = 36
LOCAL_KV_HEADS = 2
HEAD_DUPLICATES = 1
N_TP = 4


def layout(key):
    key = jax.random.fold_in(key, 11)
    brief_key, long_key, page_key = jax.random.split(key, 3)
    brief_lengths = jax.random.randint(brief_key, (INSTANCE_COUNT, DECODE_REQUESTS), 1, 2 * PAGE_TOKENS)
    longest = jax.random.randint(long_key, (INSTANCE_COUNT, 1), 0, DECODE_REQUESTS)
    slot_ids = jnp.arange(DECODE_REQUESTS)[None, :]
    cache_lengths = jnp.where(slot_ids == longest, MAXP * PAGE_TOKENS, brief_lengths).astype(jnp.int32)
    page_counts = (cache_lengths + PAGE_TOKENS - 1) // PAGE_TOKENS
    offsets = jnp.cumsum(page_counts, axis=1) - page_counts
    orders = jax.vmap(lambda k: jax.random.permutation(k, REPLICA_PAGES))(jax.random.split(page_key, INSTANCE_COUNT))
    page_index = (offsets[:, :, None] + jnp.arange(MAXP)[None, None, :]) % REPLICA_PAGES
    pages_table = jnp.take_along_axis(orders, page_index.reshape(INSTANCE_COUNT, DECODE_REQUESTS * MAXP), axis=1)
    return (cache_lengths, pages_table.reshape(INSTANCE_COUNT, DECODE_REQUESTS, MAXP).astype(jnp.int32))


def cache_base(key):
    random_seed_key = jax.random.fold_in(key, 23)
    return jax.random.truncated_normal(random_seed_key, -6.0, 6.0, (INSTANCE_COUNT, REPLICA_PAGES * PAGE_TOKENS, KEY_VALUE_HEADS, 2, HEAD_SIZE), jnp.float32)


def draw_lengths(key, part):
    cache_lengths, pages_table = layout(key)
    return cache_lengths.reshape(INSTANCE_COUNT * DECODE_REQUESTS)


def draw_block_table(key, part):
    cache_lengths, pages_table = layout(key)
    return pages_table.reshape(INSTANCE_COUNT * DECODE_REQUESTS, MAXP)


def draw_kv_cache(key, part):
    keys_base = cache_base(key)
    head_index = np.arange(N_TP)[:, None] // HEAD_DUPLICATES * LOCAL_KV_HEADS + np.arange(LOCAL_KV_HEADS)[None, :]
    spread = keys_base[:, :, head_index.reshape(-1)]
    return spread.reshape(INSTANCE_COUNT * REPLICA_PAGES * PAGE_TOKENS, N_TP * LOCAL_KV_HEADS * 2 * HEAD_SIZE).astype(jnp.bfloat16)


def draw_queries(key, part):
    key = jax.random.fold_in(key, 7)
    drawn = jax.random.truncated_normal(key, -6.0, 6.0, (INSTANCE_COUNT, DECODE_REQUESTS, QUERY_HEADS, HEAD_SIZE), jnp.float32)
    return drawn.reshape(INSTANCE_COUNT * DECODE_REQUESTS, QUERY_HEADS * HEAD_SIZE).astype(jnp.bfloat16)


def with_ends(values, rng, low, high):
    spot = [jax.random.randint(jax.random.fold_in(rng, axis), (), 0, length) for axis, length in enumerate(values.shape)]
    main_axis = values.shape.index(max(values.shape))
    next_to = spot[:main_axis] + [(spot[main_axis] + 1) % values.shape[main_axis]] + spot[main_axis + 1:]
    return values.at[tuple(spot)].set(low).at[tuple(next_to)].set(high)


def block_scale(own_key, extent, pieces, smallest, top_value):
    gain = 1.0
    for axis_at, parts in pieces:
        heights = jax.random.uniform(jax.random.fold_in(jax.random.fold_in(own_key, 6), axis_at), (parts,), jnp.float32, smallest / len(pieces), top_value / len(pieces))
        gain = gain * jnp.repeat(jnp.exp(heights), extent[axis_at] // parts).reshape((-1,) + (1,) * (len(extent) - 1 - axis_at))
    return gain


def noise(own_key, dims, scale, most, pieces=(), kind=jnp.bfloat16):
    drawn = jax.random.normal(own_key, dims, jnp.float32) * scale
    if len(pieces) > 0:
        drawn = block_scale(own_key, dims, pieces, -0.22, 0.18) * drawn
    return jnp.clip(drawn, min=-most, max=most).astype(kind)


def setup_inputs(seed: int = 0) -> dict:
    arg_keys = jax.random.split(jax.random.key(seed), 8)
    return {
        "span_hidden": noise(arg_keys[0], (INSTANCE_COUNT * PREFILL_TOKENS, MODEL_WIDTH), 1.0, 6.0, ((0, 8), (1, 4))),
        "key_value_weight": noise(arg_keys[1], (MODEL_WIDTH, KEY_VALUE_HEADS * 2 * HEAD_SIZE), MODEL_WIDTH ** -0.5, 0.0625, ((0, 4),)),
        "queries": draw_queries(jax.random.fold_in(arg_keys[7], 71), 0),
        "kv_cache": draw_kv_cache(jax.random.fold_in(arg_keys[7], 71), 0),
        "block_table": draw_block_table(jax.random.fold_in(arg_keys[7], 71), 0),
        "lengths": draw_lengths(jax.random.fold_in(arg_keys[7], 71), 0),
        "placement": with_ends(jax.random.randint(arg_keys[6], (INSTANCE_COUNT,), 0, INSTANCE_COUNT * DECODE_REQUESTS), jax.random.fold_in(arg_keys[6], 1), 0, (INSTANCE_COUNT * DECODE_REQUESTS) - 1).astype(jnp.int32),
    }


def cache_visibility(pages_table, cache_lengths, pool_pages):
    page_slots = pages_table.shape[1]
    matched = pages_table[:, :, None] == jnp.arange(pool_pages, dtype=jnp.int32)[None, None, :]
    position = jnp.arange(page_slots, dtype=jnp.int32)[:, None] * PAGE_TOKENS + jnp.arange(PAGE_TOKENS, dtype=jnp.int32)[None, :]
    inside = position[None, :, :] < cache_lengths[:, None, None]
    visible = jnp.any(matched[:, :, :, None] & inside[:, :, None, :], axis=1)
    return visible.reshape(pages_table.shape[0], pool_pages * PAGE_TOKENS)


def reference(span_hidden, key_value_weight, queries, kv_cache, block_table, lengths, placement):
    fresh_tokens = jnp.dot(span_hidden, key_value_weight, preferred_element_type=jnp.float32).astype(jnp.bfloat16)
    fresh_tokens = fresh_tokens.reshape(INSTANCE_COUNT * PREFILL_TOKENS, KEY_VALUE_HEADS, 2, HEAD_SIZE).astype(jnp.float32)
    request_slot_index = (np.arange(KEY_VALUE_HEADS) // LOCAL_KV_HEADS) * HEAD_DUPLICATES
    nested_index = np.arange(KEY_VALUE_HEADS) % LOCAL_KV_HEADS
    cache = kv_cache.reshape(INSTANCE_COUNT, REPLICA_PAGES * PAGE_TOKENS, N_TP, LOCAL_KV_HEADS, 2, HEAD_SIZE)[:, :, request_slot_index, nested_index]
    owner_rows = jnp.repeat(placement, PREFILL_TOKENS)
    query_full_batch = queries.reshape(INSTANCE_COUNT, DECODE_REQUESTS, KEY_VALUE_HEADS, QUERY_HEADS // KEY_VALUE_HEADS, HEAD_SIZE)
    table_all = block_table.reshape(INSTANCE_COUNT, DECODE_REQUESTS, MAXP)
    length_all = lengths.reshape(INSTANCE_COUNT, DECODE_REQUESTS)
    scale_factor = HEAD_SIZE ** -0.5

    def one_replica(items):
        replica, query_rows, cache_rows, pages_table, cache_lengths = items
        request_ids = replica * DECODE_REQUESTS + jnp.arange(DECODE_REQUESTS, dtype=jnp.int32)
        seen_cache = cache_visibility(pages_table, cache_lengths, REPLICA_PAGES)
        seen_fresh = owner_rows[None, :] == request_ids[:, None]
        visible = jnp.concatenate([seen_cache, seen_fresh], axis=1)
        cache_f = cache_rows.astype(jnp.float32)
        key_rows = jnp.concatenate([cache_f[:, :, 0], fresh_tokens[:, :, 0]], axis=0)
        value_rows = jnp.concatenate([cache_f[:, :, 1], fresh_tokens[:, :, 1]], axis=0)
        scores = jnp.einsum('rhgd,nhd->rhgn', query_rows.astype(jnp.float32), key_rows, precision=lax.Precision.HIGHEST) * scale_factor
        scores = jnp.where(visible[:, None, None, :], scores, -jnp.inf)
        top = jnp.max(scores, axis=-1, keepdims=True)
        probs = jnp.exp(scores - top)
        totals = jnp.sum(probs, axis=-1)
        weights = probs.astype(jnp.bfloat16).astype(jnp.float32)
        summed = jnp.einsum('rhgn,nhd->rhgd', weights, value_rows, precision=lax.Precision.HIGHEST)
        result = summed / totals[..., None]
        return result.reshape(DECODE_REQUESTS, QUERY_HEADS * HEAD_SIZE).astype(jnp.bfloat16)

    outputs = lax.map(one_replica, (jnp.arange(INSTANCE_COUNT, dtype=jnp.int32), query_full_batch, cache, table_all, length_all))
    return outputs.reshape(INSTANCE_COUNT * DECODE_REQUESTS, QUERY_HEADS * HEAD_SIZE)
```

```python
import functools

import jax
import jax.numpy as jnp
from jax import lax
from jax.experimental import pallas as pl
from jax.experimental.pallas import tpu as pltpu
from jax.sharding import PartitionSpec as P

HEAD_SIZE = 128
PAGE_TOKENS = 128
MESH = pl.DeviceIdType.MESH
HIDDEN = -1e30
CHUNKS = 4
NT = (((1,), (1,)), ((), ()))
NN = (((1,), (0,)), ((), ()))


def dot(a, b, dims):
    return lax.dot_general(a, b, dims, preferred_element_type=jnp.float32)


def split(value):
    high = value.astype(jnp.bfloat16)
    return high, (value - high.astype(jnp.float32)).astype(jnp.bfloat16)


def spread(rows, heads):
    if heads == 1:
        return rows
    each = rows.shape[0] // heads
    owner = lax.broadcasted_iota(jnp.int32, rows.shape, 0) // each
    wide = rows.astype(jnp.float32)
    parts = [jnp.where(owner == h, wide, 0.0) for h in range(heads)]
    return jnp.concatenate(parts, axis=1).astype(jnp.bfloat16)


def gather_blocks(rows, heads):
    if heads == 1:
        return rows
    each = rows.shape[0] // heads
    shape = (rows.shape[0], HEAD_SIZE)
    owner = lax.broadcasted_iota(jnp.int32, shape, 0) // each
    result = rows[:, :HEAD_SIZE]
    for h in range(1, heads):
        result = jnp.where(owner == h, rows[:, h * HEAD_SIZE:(h + 1) * HEAD_SIZE], result)
    return result


def kernel(
    sizes,
    placement, table, lengths, q_ref, x_hbm, w_hbm, cache_hbm,
    out_ref,
    x_v, w_v, cache_v, chosen, q_land, q_all, qt, s_part, s_land, p_all, ub, o_part, o_land,
    state, c_out, c_max, c_sum,
    local_sem, a_send, a_recv, t_send, t_recv, e_send, e_recv,
):
    n_role, n_rep, n_tp = sizes
    n_replica = n_role * n_rep
    scale = HEAD_SIZE ** -0.5
    requests, rows = q_ref.shape[0], q_ref.shape[1]
    features = x_v.shape[1]
    local_heads = cache_v.shape[2] // (2 * HEAD_SIZE)
    pairs = w_v.shape[1] // (4 * HEAD_SIZE)
    pair_rows = n_tp * rows // pairs
    pair_slots = pair_rows // rows
    piece = features // CHUNKS
    slots = table.shape[1]

    replica = lax.axis_index("role") * n_rep + lax.axis_index("rep")
    t = lax.axis_index("tp")

    def on_replica(i):
        return (i // n_rep, lax.rem(i, n_rep), t)

    def on_tp(i):
        return (lax.axis_index("role"), lax.axis_index("rep"), i)

    def others(me, count):
        return [(d, lax.rem(me + d, count)) for d in range(1, count)]

    replicas = others(replica, n_replica)
    columns = others(t, n_tp)

    half = cache_v.shape[0] // 2
    cache_copies = [
        pltpu.make_async_copy(
            cache_hbm.at[pl.ds(h * half, half)], cache_v.at[pl.ds(h * half, half)], local_sem.at[h]
        )
        for h in range(2)
    ]
    w_copies = [
        pltpu.make_async_copy(
            w_hbm.at[pl.ds(c * piece, piece)], w_v.at[pl.ds(c * piece, piece)], local_sem.at[2 + c]
        )
        for c in range(CHUNKS)
    ]
    x_copy = pltpu.make_async_copy(x_hbm, x_v, local_sem.at[2 + CHUNKS])
    for copy in cache_copies + w_copies + [x_copy]:
        copy.start()

    barrier = pltpu.get_barrier_semaphore()
    for _, i in replicas:
        pl.semaphore_signal(barrier, inc=1, device_id=on_replica(i), device_id_type=MESH)
    for _, i in columns:
        pl.semaphore_signal(barrier, inc=1, device_id=on_tp(i), device_id_type=MESH)
    for i in range(n_replica):
        chosen[i] = q_ref[lax.rem(placement[i], requests)]
    pl.semaphore_wait(barrier, n_replica + n_tp - 2)

    pending = []

    def send(source, land, slot, peers, device, send_sem, recv_sem):
        for d, i in peers:
            copy = pltpu.make_async_remote_copy(
                src_ref=source(i), dst_ref=land.at[slot],
                send_sem=send_sem.at[d], recv_sem=recv_sem.at[slot],
                device_id=device(i), device_id_type=MESH,
            )
            copy.start()
            pending.append(copy)

    def receive(land, peers, device, send_sem, recv_sem):
        for d, i in peers:
            pltpu.make_async_remote_copy(
                src_ref=land.at[i], dst_ref=land.at[i],
                send_sem=send_sem.at[d], recv_sem=recv_sem.at[i],
                device_id=device(i), device_id_type=MESH,
            ).wait_recv()

    send(lambda i: chosen.at[i], q_land, replica, replicas, on_replica, a_send, a_recv)
    q_land[replica] = chosen[replica]

    def cache_request(k):
        blocks = [
            cache_v[table[k, j]]
            for j in range(slots)
        ]
        block = jnp.concatenate(blocks, axis=0)

        def take(which):
            return jnp.concatenate(
                [
                    block[:, (2 * h + which) * HEAD_SIZE:(2 * h + which + 1) * HEAD_SIZE]
                    for h in range(local_heads)
                ],
                axis=1,
            )

        scores = dot(spread(q_ref[k], local_heads), take(0), NT) * scale
        seen = lax.broadcasted_iota(jnp.int32, scores.shape, 1) < lengths[k]
        scores = jnp.where(seen, scores, HIDDEN)
        top = jnp.max(scores, axis=1, keepdims=True)
        probs = jnp.where(seen, jnp.exp(scores - top), 0.0)
        total = jnp.sum(probs, axis=1, keepdims=True)
        summed = dot(probs.astype(jnp.bfloat16), take(1), NN)
        c_out[k] = gather_blocks(summed, local_heads)
        c_max[k] = jnp.broadcast_to(top, (rows, HEAD_SIZE))
        c_sum[k] = jnp.broadcast_to(total, (rows, HEAD_SIZE))

    def cache_part(first, last):
        def body(step, carry):
            for u in range(2):
                cache_request(first + 2 * step + u)
            return carry

        lax.fori_loop(0, (last - first) // 2, body, 0)

    for copy in cache_copies:
        copy.wait()
    cache_part(0, requests // 2)

    receive(q_land, replicas, on_replica, a_send, a_recv)
    q_all[t] = q_land[lax.div(placement[replica], requests)]
    send(lambda i: q_all.at[t], q_all, t, columns, on_tp, t_send.at[0], t_recv.at[0])
    cache_part(requests // 2, 3 * requests // 4)
    receive(q_all, columns, on_tp, t_send.at[0], t_recv.at[0])

    pair_q = q_all[...].reshape(pairs, pair_rows, HEAD_SIZE)
    wide_q = [spread(pair_q[g], 2) for g in range(pairs)]

    def weight(rows_at, g, which):
        left = (4 * g + which) * HEAD_SIZE
        right = (4 * g + 2 + which) * HEAD_SIZE
        return jnp.concatenate(
            [w_v[rows_at, left:left + HEAD_SIZE], w_v[rows_at, right:right + HEAD_SIZE]], axis=1
        )

    for c in range(CHUNKS):
        w_copies[c].wait()
        at = pl.ds(c * piece, piece)
        for g in range(pairs):
            high, low = split(dot(wide_q[g], weight(at, g, 0), NT))
            qt[g, 0, :, at] = high
            qt[g, 1, :, at] = low
    x_copy.wait()
    both = dot(qt[...].reshape(pairs * 2 * pair_rows, features), x_v[...], NT)
    tokens = both.shape[1]
    both = both.reshape(pairs, 2, pair_rows, tokens)
    s_part[...] = (both[:, 0] + both[:, 1]).reshape(n_tp, rows, tokens)
    send(lambda i: s_part.at[i], s_land, t, columns, on_tp, t_send.at[1], t_recv.at[1])
    cache_part(3 * requests // 4, requests)
    receive(s_land, columns, on_tp, t_send.at[1], t_recv.at[1])

    scores = s_part[t]
    for _, i in columns:
        scores = scores + s_land[i]
    scores = scores * scale
    top = jnp.max(scores, axis=1, keepdims=True)
    probs = jnp.exp(scores - top)
    p_all[t] = probs.astype(jnp.bfloat16)
    send(lambda i: p_all.at[t], p_all, t, columns, on_tp, t_send.at[2], t_recv.at[2])
    state[replica, 1] = jnp.broadcast_to(top, (rows, HEAD_SIZE))
    state[replica, 2] = jnp.broadcast_to(jnp.sum(probs, axis=1, keepdims=True), (rows, HEAD_SIZE))
    receive(p_all, columns, on_tp, t_send.at[2], t_recv.at[2])

    weights = p_all[...].reshape(n_tp * rows, tokens)
    for c in range(CHUNKS):
        at = pl.ds(c * piece, piece)
        high, low = split(dot(weights, x_v[:, at], NN))
        ub[:, 0, :, at] = high.reshape(pairs, pair_rows, piece)
        ub[:, 1, :, at] = low.reshape(pairs, pair_rows, piece)
    for g in range(pairs):
        both = dot(ub[g].reshape(2 * pair_rows, features), weight(slice(None), g, 1), NN)
        both = gather_blocks(both[:pair_rows] + both[pair_rows:], 2)
        o_part[g * pair_slots:(g + 1) * pair_slots] = both.reshape(pair_slots, rows, HEAD_SIZE)
    send(lambda i: o_part.at[i], o_land, t, columns, on_tp, t_send.at[3], t_recv.at[3])
    receive(o_land, columns, on_tp, t_send.at[3], t_recv.at[3])
    summed = o_part[t]
    for _, i in columns:
        summed = summed + o_land[i]
    state[replica, 0] = summed

    send(lambda i: state.at[replica], state, replica, replicas, on_replica, e_send, e_recv)
    receive(state, replicas, on_replica, e_send, e_recv)

    def combine(k, carry):
        request = jnp.full((rows, HEAD_SIZE), replica * requests + k, jnp.int32)
        hits = [request == placement[i] for i in range(n_replica)]
        top = c_max[k]
        for i in range(n_replica):
            top = jnp.maximum(top, jnp.where(hits[i], state[i, 1], HIDDEN))
        factor = jnp.exp(c_max[k] - top)
        summed = c_out[k] * factor
        total = c_sum[k] * factor
        for i in range(n_replica):
            factor = jnp.where(hits[i], jnp.exp(state[i, 1] - top), 0.0)
            summed = summed + state[i, 0] * factor
            total = total + state[i, 2] * factor
        out_ref[k] = (summed / total).astype(out_ref.dtype)
        return carry

    lax.fori_loop(0, requests, combine, 0)
    for copy in pending:
        copy.wait_send()


def local(sizes, span_hidden, key_value_weight, queries, kv_cache, block_table, lengths, placement):
    n_role, n_rep, n_tp = sizes
    n_replica = n_role * n_rep
    requests = queries.shape[0]
    heads = queries.shape[1] // HEAD_SIZE
    rows = max(heads, 16)
    tokens, features = span_hidden.shape
    pairs = key_value_weight.shape[1] // (4 * HEAD_SIZE)
    pair_rows = n_tp * rows // pairs
    pool = kv_cache.reshape(-1, PAGE_TOKENS, kv_cache.shape[1])
    q = queries.reshape(requests, heads, HEAD_SIZE)
    if rows > heads:
        q = jnp.pad(q, ((0, 0), (0, rows - heads), (0, 0)))
    bf16, f32 = jnp.bfloat16, jnp.float32
    smem = pl.BlockSpec(memory_space=pltpu.SMEM)
    vmem = pl.BlockSpec(memory_space=pltpu.VMEM)
    hbm = pl.BlockSpec(memory_space=pl.ANY)
    dma = pltpu.SemaphoreType.DMA
    out = pl.pallas_call(
        functools.partial(kernel, sizes),
        out_shape=jax.ShapeDtypeStruct((requests, rows, HEAD_SIZE), bf16),
        in_specs=[smem, smem, smem, vmem, hbm, hbm, hbm],
        out_specs=vmem,
        scratch_shapes=[
            pltpu.VMEM(span_hidden.shape, bf16),
            pltpu.VMEM(key_value_weight.shape, bf16),
            pltpu.VMEM(pool.shape, bf16),
            pltpu.VMEM((n_replica, rows, HEAD_SIZE), bf16),
            pltpu.VMEM((n_replica, rows, HEAD_SIZE), bf16),
            pltpu.VMEM((n_tp, rows, HEAD_SIZE), bf16),
            pltpu.VMEM((pairs, 2, pair_rows, features), bf16),
            pltpu.VMEM((n_tp, rows, tokens), f32),
            pltpu.VMEM((n_tp, rows, tokens), f32),
            pltpu.VMEM((n_tp, rows, tokens), bf16),
            pltpu.VMEM((pairs, 2, pair_rows, features), bf16),
            pltpu.VMEM((n_tp, rows, HEAD_SIZE), f32),
            pltpu.VMEM((n_tp, rows, HEAD_SIZE), f32),
            pltpu.VMEM((n_replica, 3, rows, HEAD_SIZE), f32),
            pltpu.VMEM((requests, rows, HEAD_SIZE), f32),
            pltpu.VMEM((requests, rows, HEAD_SIZE), f32),
            pltpu.VMEM((requests, rows, HEAD_SIZE), f32),
            dma((3 + CHUNKS,)),
            dma((n_replica,)),
            dma((n_replica,)),
            dma((4, n_tp)),
            dma((4, n_tp)),
            dma((n_replica,)),
            dma((n_replica,)),
        ],
        compiler_params=pltpu.CompilerParams(
            collective_id=0, has_side_effects=True, vmem_limit_bytes=60 * 1024 * 1024
        ),
    )(placement, block_table, lengths, q, span_hidden, key_value_weight, pool)
    return out[:, :heads].reshape(requests, heads * HEAD_SIZE)


def solution(mesh):
    placed = (
        P(("role", "rep"), "tp"),
        P("tp", None),
        P(("role", "rep"), "tp"),
        P(("role", "rep"), "tp"),
        P(("role", "rep"), None),
        P(("role", "rep")),
        P(),
    )
    sizes = (mesh.shape["role"], mesh.shape["rep"], mesh.shape["tp"])
    return jax.shard_map(
        functools.partial(local, sizes),
        mesh=mesh, in_specs=placed, out_specs=P(("role", "rep"), "tp"), check_vma=False,
    )
```

```python
import functools

import jax
import jax.numpy as jnp
from jax import lax
from jax.experimental import pallas as pl
from jax.experimental.pallas import tpu as pltpu
from jax.sharding import PartitionSpec as P

HEAD_SIZE = 128
PAGE_TOKENS = 128
MESH = pl.DeviceIdType.MESH
HIDDEN = -1e30
CHUNKS = 4
NT = (((1,), (1,)), ((), ()))
NN = (((1,), (0,)), ((), ()))


def dot(a, b, dims):
    return lax.dot_general(a, b, dims, preferred_element_type=jnp.float32)


def split(value):
    high = value.astype(jnp.bfloat16)
    return high, (value - high.astype(jnp.float32)).astype(jnp.bfloat16)


def spread(rows, heads):
    if heads == 1:
        return rows
    each = rows.shape[0] // heads
    owner = lax.broadcasted_iota(jnp.int32, rows.shape, 0) // each
    wide = rows.astype(jnp.float32)
    parts = [jnp.where(owner == h, wide, 0.0) for h in range(heads)]
    return jnp.concatenate(parts, axis=1).astype(jnp.bfloat16)


def gather_blocks(rows, heads):
    if heads == 1:
        return rows
    each = rows.shape[0] // heads
    shape = (rows.shape[0], HEAD_SIZE)
    owner = lax.broadcasted_iota(jnp.int32, shape, 0) // each
    result = rows[:, :HEAD_SIZE]
    for h in range(1, heads):
        result = jnp.where(owner == h, rows[:, h * HEAD_SIZE:(h + 1) * HEAD_SIZE], result)
    return result


def kernel(
    sizes,
    placement, table, lengths, q_ref, x_hbm, w_hbm, cache_hbm,
    out_ref,
    x_v, w_v, cache_v, q_rows, chosen, q_land, q_all, qt, s_part, s_land, p_all, ub, o_part, o_land,
    state, marks, c_out, c_max, c_sum,
    local_sem, a_send, a_recv, t_send, t_recv, m_send, m_recv, e_send, e_recv,
):
    n_role, n_rep, n_tp = sizes
    n_replica = n_role * n_rep
    scale = HEAD_SIZE ** -0.5
    requests, rows = q_rows.shape[0], q_rows.shape[1]
    heads = q_ref.shape[1] // HEAD_SIZE
    features = x_v.shape[1]
    local_heads = cache_v.shape[2] // (2 * HEAD_SIZE)
    pairs = w_v.shape[1] // (4 * HEAD_SIZE)
    pair_rows = n_tp * rows // pairs
    pair_slots = pair_rows // rows
    piece = features // CHUNKS
    slots = table.shape[0]

    replica = lax.axis_index("role") * n_rep + lax.axis_index("rep")
    t = lax.axis_index("tp")

    def on_replica(i):
        return (i // n_rep, lax.rem(i, n_rep), t)

    def on_tp(i):
        return (lax.axis_index("role"), lax.axis_index("rep"), i)

    def others(me, count):
        return [(d, lax.rem(me + d, count)) for d in range(1, count)]

    replicas = others(replica, n_replica)
    columns = others(t, n_tp)

    barrier = pltpu.get_barrier_semaphore()
    for _, i in replicas:
        pl.semaphore_signal(barrier, inc=1, device_id=on_replica(i), device_id_type=MESH)
    for _, i in columns:
        pl.semaphore_signal(barrier, inc=1, device_id=on_tp(i), device_id_type=MESH)
    half = cache_v.shape[0] // 2
    cache_copies = [
        pltpu.make_async_copy(
            cache_hbm.at[pl.ds(h * half, half)], cache_v.at[pl.ds(h * half, half)], local_sem.at[h]
        )
        for h in range(2)
    ]
    w_copies = [
        pltpu.make_async_copy(
            w_hbm.at[pl.ds(c * piece, piece)], w_v.at[pl.ds(c * piece, piece)], local_sem.at[2 + c]
        )
        for c in range(CHUNKS)
    ]
    x_copy = pltpu.make_async_copy(x_hbm, x_v, local_sem.at[2 + CHUNKS])
    for copy in cache_copies + w_copies + [x_copy]:
        copy.start()

    if rows > heads:
        q_rows[...] = jnp.zeros_like(q_rows)
    for h in range(heads):
        q_rows[:, h, :] = q_ref[:, h * HEAD_SIZE:(h + 1) * HEAD_SIZE].astype(jnp.float32)
    for i in range(n_replica):
        chosen[i] = q_rows[lax.rem(placement[i], requests)].astype(jnp.bfloat16)
    pl.semaphore_wait(barrier, n_replica + n_tp - 2)

    pending = []

    def send(source, land, slot, peers, device, send_sem, recv_sem):
        for d, i in peers:
            copy = pltpu.make_async_remote_copy(
                src_ref=source(i), dst_ref=land.at[slot],
                send_sem=send_sem.at[d], recv_sem=recv_sem.at[slot],
                device_id=device(i), device_id_type=MESH,
            )
            copy.start()
            pending.append(copy)

    def receive(land, peers, device, send_sem, recv_sem):
        for d, i in peers:
            pltpu.make_async_remote_copy(
                src_ref=land.at[i], dst_ref=land.at[i],
                send_sem=send_sem.at[d], recv_sem=recv_sem.at[i],
                device_id=device(i), device_id_type=MESH,
            ).wait_recv()

    send(lambda i: chosen.at[i], q_land, replica, replicas, on_replica, a_send, a_recv)
    q_land[replica] = chosen[replica]

    def cache_request(k):
        blocks = [
            cache_v[table[j, k]]
            for j in range(slots)
        ]
        block = jnp.concatenate(blocks, axis=0)

        def take(which):
            return jnp.concatenate(
                [
                    block[:, (2 * h + which) * HEAD_SIZE:(2 * h + which + 1) * HEAD_SIZE]
                    for h in range(local_heads)
                ],
                axis=1,
            )

        scores = dot(spread(q_rows[k].astype(jnp.bfloat16), local_heads), take(0), NT) * scale
        seen = lax.broadcasted_iota(jnp.int32, scores.shape, 1) < lengths[k]
        scores = jnp.where(seen, scores, HIDDEN)
        top = jnp.max(scores, axis=1, keepdims=True)
        probs = jnp.where(seen, jnp.exp(scores - top), 0.0)
        total = jnp.sum(probs, axis=1, keepdims=True)
        summed = dot(probs.astype(jnp.bfloat16), take(1), NN)
        c_out[k] = gather_blocks(summed, local_heads)
        c_max[k] = jnp.broadcast_to(top, (rows, HEAD_SIZE))
        c_sum[k] = jnp.broadcast_to(total, (rows, HEAD_SIZE))

    def cache_part(first, last):
        def body(step, carry):
            for u in range(2):
                cache_request(first + 2 * step + u)
            return carry

        lax.fori_loop(0, (last - first) // 2, body, 0)

    for copy in cache_copies:
        copy.wait()
    cache_part(0, requests // 2)

    receive(q_land, replicas, on_replica, a_send, a_recv)
    q_all[t] = q_land[lax.div(placement[replica], requests)]
    send(lambda i: q_all.at[t], q_all, t, columns, on_tp, t_send.at[0], t_recv.at[0])
    cache_part(requests // 2, 3 * requests // 4)
    receive(q_all, columns, on_tp, t_send.at[0], t_recv.at[0])

    pair_q = q_all[...].reshape(pairs, pair_rows, HEAD_SIZE)
    wide_q = [spread(pair_q[g], 2) for g in range(pairs)]

    def weight(rows_at, g, which):
        left = (4 * g + which) * HEAD_SIZE
        right = (4 * g + 2 + which) * HEAD_SIZE
        return jnp.concatenate(
            [w_v[rows_at, left:left + HEAD_SIZE], w_v[rows_at, right:right + HEAD_SIZE]], axis=1
        )

    for c in range(CHUNKS):
        w_copies[c].wait()
        at = pl.ds(c * piece, piece)
        for g in range(pairs):
            high, low = split(dot(wide_q[g], weight(at, g, 0), NT))
            qt[g, 0, :, at] = high
            qt[g, 1, :, at] = low
    x_copy.wait()
    both = dot(qt[...].reshape(pairs * 2 * pair_rows, features), x_v[...], NT)
    tokens = both.shape[1]
    both = both.reshape(pairs, 2, pair_rows, tokens)
    s_part[...] = (both[:, 0] + both[:, 1]).reshape(n_tp, rows, tokens)
    send(lambda i: s_part.at[i], s_land, t, columns, on_tp, t_send.at[1], t_recv.at[1])
    cache_part(3 * requests // 4, requests)
    receive(s_land, columns, on_tp, t_send.at[1], t_recv.at[1])

    scores = s_part[t]
    for _, i in columns:
        scores = scores + s_land[i]
    scores = scores * scale
    top = jnp.max(scores, axis=1, keepdims=True)
    probs = jnp.exp(scores - top)
    p_all[t] = probs.astype(jnp.bfloat16)
    send(lambda i: p_all.at[t], p_all, t, columns, on_tp, t_send.at[2], t_recv.at[2])
    marks[replica, 0] = jnp.broadcast_to(top, (rows, HEAD_SIZE))
    marks[replica, 1] = jnp.broadcast_to(jnp.sum(probs, axis=1, keepdims=True), (rows, HEAD_SIZE))
    send(lambda i: marks.at[replica], marks, replica, replicas, on_replica, m_send, m_recv)
    receive(p_all, columns, on_tp, t_send.at[2], t_recv.at[2])

    weights = p_all[...].reshape(n_tp * rows, tokens)
    for c in range(CHUNKS):
        at = pl.ds(c * piece, piece)
        high, low = split(dot(weights, x_v[:, at], NN))
        ub[:, 0, :, at] = high.reshape(pairs, pair_rows, piece)
        ub[:, 1, :, at] = low.reshape(pairs, pair_rows, piece)
    for g in range(pairs):
        both = dot(ub[g].reshape(2 * pair_rows, features), weight(slice(None), g, 1), NN)
        both = gather_blocks(both[:pair_rows] + both[pair_rows:], 2)
        o_part[g * pair_slots:(g + 1) * pair_slots] = both.reshape(pair_slots, rows, HEAD_SIZE)
    send(lambda i: o_part.at[i], o_land, t, columns, on_tp, t_send.at[3], t_recv.at[3])
    receive(o_land, columns, on_tp, t_send.at[3], t_recv.at[3])
    summed = o_part[t]
    for _, i in columns:
        summed = summed + o_land[i]
    state[replica] = summed

    send(lambda i: state.at[replica], state, replica, replicas, on_replica, e_send, e_recv)
    receive(marks, replicas, on_replica, m_send, m_recv)
    receive(state, replicas, on_replica, e_send, e_recv)

    def combine(k, carry):
        request = jnp.full((rows, HEAD_SIZE), replica * requests + k, jnp.int32)
        hits = [request == placement[i] for i in range(n_replica)]
        top = c_max[k]
        for i in range(n_replica):
            top = jnp.maximum(top, jnp.where(hits[i], marks[i, 0], HIDDEN))
        factor = jnp.exp(c_max[k] - top)
        summed = c_out[k] * factor
        total = c_sum[k] * factor
        for i in range(n_replica):
            factor = jnp.where(hits[i], jnp.exp(marks[i, 0] - top), 0.0)
            summed = summed + state[i] * factor
            total = total + marks[i, 1] * factor
        c_out[k] = summed / total
        return carry

    lax.fori_loop(0, requests, combine, 0)
    for h in range(heads):
        out_ref[:, h * HEAD_SIZE:(h + 1) * HEAD_SIZE] = c_out[:, h, :].astype(out_ref.dtype)
    for copy in pending:
        copy.wait_send()


def local(sizes, span_hidden, key_value_weight, queries, kv_cache, block_table, lengths, placement):
    n_role, n_rep, n_tp = sizes
    n_replica = n_role * n_rep
    requests = queries.shape[0]
    heads = queries.shape[1] // HEAD_SIZE
    rows = max(heads, 16)
    tokens, features = span_hidden.shape
    pairs = key_value_weight.shape[1] // (4 * HEAD_SIZE)
    pair_rows = n_tp * rows // pairs
    pool = kv_cache.reshape(-1, PAGE_TOKENS, kv_cache.shape[1])
    bf16, f32 = jnp.bfloat16, jnp.float32
    smem = pl.BlockSpec(memory_space=pltpu.SMEM)
    vmem = pl.BlockSpec(memory_space=pltpu.VMEM)
    hbm = pl.BlockSpec(memory_space=pl.ANY)
    dma = pltpu.SemaphoreType.DMA
    return pl.pallas_call(
        functools.partial(kernel, sizes),
        out_shape=jax.ShapeDtypeStruct(queries.shape, bf16),
        in_specs=[smem, smem, smem, vmem, hbm, hbm, hbm],
        out_specs=vmem,
        scratch_shapes=[
            pltpu.VMEM(span_hidden.shape, bf16),
            pltpu.VMEM(key_value_weight.shape, bf16),
            pltpu.VMEM(pool.shape, bf16),
            pltpu.VMEM((requests, rows, HEAD_SIZE), f32),
            pltpu.VMEM((n_replica, rows, HEAD_SIZE), bf16),
            pltpu.VMEM((n_replica, rows, HEAD_SIZE), bf16),
            pltpu.VMEM((n_tp, rows, HEAD_SIZE), bf16),
            pltpu.VMEM((pairs, 2, pair_rows, features), bf16),
            pltpu.VMEM((n_tp, rows, tokens), f32),
            pltpu.VMEM((n_tp, rows, tokens), f32),
            pltpu.VMEM((n_tp, rows, tokens), bf16),
            pltpu.VMEM((pairs, 2, pair_rows, features), bf16),
            pltpu.VMEM((n_tp, rows, HEAD_SIZE), f32),
            pltpu.VMEM((n_tp, rows, HEAD_SIZE), f32),
            pltpu.VMEM((n_replica, rows, HEAD_SIZE), f32),
            pltpu.VMEM((n_replica, 2, rows, HEAD_SIZE), f32),
            pltpu.VMEM((requests, rows, HEAD_SIZE), f32),
            pltpu.VMEM((requests, rows, HEAD_SIZE), f32),
            pltpu.VMEM((requests, rows, HEAD_SIZE), f32),
            dma((3 + CHUNKS,)),
            dma((n_replica,)),
            dma((n_replica,)),
            dma((4, n_tp)),
            dma((4, n_tp)),
            dma((n_replica,)),
            dma((n_replica,)),
            dma((n_replica,)),
            dma((n_replica,)),
        ],
        compiler_params=pltpu.CompilerParams(
            collective_id=0, has_side_effects=True, vmem_limit_bytes=60 * 1024 * 1024
        ),
    )(placement, block_table.T, lengths, queries, span_hidden, key_value_weight, pool)


def solution(mesh):
    placed = (
        P(("role", "rep"), "tp"),
        P("tp", None),
        P(("role", "rep"), "tp"),
        P(("role", "rep"), "tp"),
        P(("role", "rep"), None),
        P(("role", "rep")),
        P(),
    )
    sizes = (mesh.shape["role"], mesh.shape["rep"], mesh.shape["tp"])
    return jax.shard_map(
        functools.partial(local, sizes),
        mesh=mesh, in_specs=placed, out_specs=P(("role", "rep"), "tp"), check_vma=False,
    )
```

```python
import functools

import jax
import jax.numpy as jnp
from jax import lax
from jax.experimental import pallas as pl
from jax.experimental.pallas import tpu as pltpu
from jax.sharding import PartitionSpec as P

HEAD_SIZE = 128
PAGE_TOKENS = 128
MESH = pl.DeviceIdType.MESH
HIDDEN = -1e30
CHUNKS = 4
NT = (((1,), (1,)), ((), ()))
NN = (((1,), (0,)), ((), ()))


def dot(a, b, dims):
    return lax.dot_general(a, b, dims, preferred_element_type=jnp.float32)


def split(value):
    high = value.astype(jnp.bfloat16)
    return high, (value - high.astype(jnp.float32)).astype(jnp.bfloat16)


def spread(rows, heads, each, first=0):
    if heads == 1:
        return rows
    owner = (lax.broadcasted_iota(jnp.int32, rows.shape, 0) + first) // each
    wide = rows.astype(jnp.float32)
    parts = [jnp.where(owner == h, wide, 0.0) for h in range(heads)]
    return jnp.concatenate(parts, axis=1).astype(jnp.bfloat16)


def gather_blocks(rows, heads, each, first=0):
    if heads == 1:
        return rows
    shape = (rows.shape[0], HEAD_SIZE)
    owner = (lax.broadcasted_iota(jnp.int32, shape, 0) + first) // each
    result = rows[:, :HEAD_SIZE]
    for h in range(1, heads):
        result = jnp.where(owner == h, rows[:, h * HEAD_SIZE:(h + 1) * HEAD_SIZE], result)
    return result


def kernel(
    sizes,
    placement, table, lengths, q_ref, x_hbm, w_hbm, cache_hbm,
    out_ref,
    x_v, w_v, cache_v, q_rows, chosen, q_land, q_all, s_part, s_land, p_all, o_part, o_land,
    state, marks, factors, c_out, c_max, c_sum,
    local_sem, a_send, a_recv, t_send, t_recv, m_send, m_recv, e_send, e_recv,
):
    n_role, n_rep, n_tp = sizes
    n_replica = n_role * n_rep
    scale = HEAD_SIZE ** -0.5
    requests, rows = q_rows.shape[0], q_rows.shape[1]
    heads = q_ref.shape[1] // HEAD_SIZE
    features = x_v.shape[1]
    local_heads = cache_v.shape[2] // (2 * HEAD_SIZE)
    pairs = w_v.shape[1] // (4 * HEAD_SIZE)
    pair_rows = n_tp * rows // pairs
    pair_slots = pair_rows // rows
    piece = features // CHUNKS
    slots = table.shape[0]

    replica = lax.axis_index("role") * n_rep + lax.axis_index("rep")
    t = lax.axis_index("tp")

    role, rep = lax.axis_index("role"), lax.axis_index("rep")

    def wrap(value, count):
        return jnp.where(value >= count, value - count, value)

    replicas = []
    for step in range(1, n_replica):
        to_role, to_rep = wrap(role + step // n_rep, n_role), wrap(rep + step % n_rep, n_rep)
        replicas.append((step, to_role * n_rep + to_rep, (to_role, to_rep, t)))
    columns = []
    for step in range(1, n_tp):
        down, up = n_tp - step, step - 1
        down = jnp.where(down <= t, down - 1, down)
        up = jnp.where(up >= t, up + 1, up)
        to_tp = jnp.where(2 * t < n_tp, down, up)
        columns.append((step, to_tp, (role, rep, to_tp)))

    barrier = pltpu.get_barrier_semaphore()
    for _, _, device in columns + replicas:
        pl.semaphore_signal(barrier, inc=1, device_id=device, device_id_type=MESH)
    half = cache_v.shape[0] // 2
    cache_copies = [
        pltpu.make_async_copy(
            cache_hbm.at[pl.ds(h * half, half)], cache_v.at[pl.ds(h * half, half)], local_sem.at[h]
        )
        for h in range(2)
    ]
    w_copies = [
        pltpu.make_async_copy(
            w_hbm.at[pl.ds(c * piece, piece)], w_v.at[pl.ds(c * piece, piece)], local_sem.at[2 + c]
        )
        for c in range(CHUNKS)
    ]
    x_copy = pltpu.make_async_copy(x_hbm, x_v, local_sem.at[2 + CHUNKS])
    for copy in cache_copies + w_copies + [x_copy]:
        copy.start()

    if rows > heads:
        q_rows[...] = jnp.zeros_like(q_rows)
    for h in range(heads):
        q_rows[:, h, :] = q_ref[:, h * HEAD_SIZE:(h + 1) * HEAD_SIZE].astype(jnp.float32)
    for i in range(n_replica):
        chosen[i] = q_rows[lax.rem(placement[i], requests)].astype(jnp.bfloat16)
    pl.semaphore_wait(barrier, n_replica + n_tp - 2)

    pending = []

    def send(source, land, slot, peers, send_sem, recv_sem):
        for d, i, device in peers:
            copy = pltpu.make_async_remote_copy(
                src_ref=source(i), dst_ref=land.at[slot],
                send_sem=send_sem.at[d], recv_sem=recv_sem.at[slot],
                device_id=device, device_id_type=MESH,
            )
            copy.start()
            pending.append(copy)

    def deliver(source, land, peer, part):
        d, i, device = peer
        copy = pltpu.make_async_remote_copy(
            src_ref=source, dst_ref=land.at[t],
            send_sem=t_send.at[part, d], recv_sem=t_recv.at[part, t],
            device_id=device, device_id_type=MESH,
        )
        copy.start()
        pending.append(copy)

    def receive(land, peers, send_sem, recv_sem):
        for d, i, device in peers:
            pltpu.make_async_remote_copy(
                src_ref=land.at[i], dst_ref=land.at[i],
                send_sem=send_sem.at[d], recv_sem=recv_sem.at[i],
                device_id=device, device_id_type=MESH,
            ).wait_recv()

    send(lambda i: chosen.at[i], q_land, replica, replicas, a_send, a_recv)
    q_land[replica] = chosen[replica]

    def cache_request(k):
        blocks = [
            cache_v[table[j, k]]
            for j in range(slots)
        ]
        block = jnp.concatenate(blocks, axis=0)

        def take(which):
            return jnp.concatenate(
                [
                    block[:, (2 * h + which) * HEAD_SIZE:(2 * h + which + 1) * HEAD_SIZE]
                    for h in range(local_heads)
                ],
                axis=1,
            )

        scores = dot(spread(q_rows[k].astype(jnp.bfloat16), local_heads, rows // local_heads), take(0), NT) * scale
        seen = lax.broadcasted_iota(jnp.int32, scores.shape, 1) < lengths[k]
        scores = jnp.where(seen, scores, HIDDEN)
        top = jnp.max(scores, axis=1, keepdims=True)
        probs = jnp.where(seen, jnp.exp(scores - top), 0.0)
        total = jnp.sum(probs, axis=1, keepdims=True)
        summed = dot(probs.astype(jnp.bfloat16), take(1), NN)
        c_out[k] = gather_blocks(summed, local_heads, rows // local_heads)
        c_max[k] = jnp.broadcast_to(top, (rows, HEAD_SIZE))
        c_sum[k] = jnp.broadcast_to(total, (rows, HEAD_SIZE))

    def cache_part(first, last):
        def body(step, carry):
            for u in range(2):
                cache_request(first + 2 * step + u)
            return carry

        lax.fori_loop(0, (last - first) // 2, body, 0)

    for copy in cache_copies:
        copy.wait()
    cache_part(0, 5 * requests // 8)

    receive(q_land, replicas, a_send, a_recv)
    q_all[t] = q_land[lax.div(placement[replica], requests)]
    send(lambda i: q_all.at[t], q_all, t, columns, t_send.at[0], t_recv.at[0])
    cache_part(5 * requests // 8, requests)
    receive(q_all, columns, t_send.at[0], t_recv.at[0])

    def weight(slot, which):
        left = (slot // pair_slots) * (4 * HEAD_SIZE) + which * HEAD_SIZE
        return jnp.concatenate(
            [
                w_v[:, pl.ds(pl.multiple_of(left + h * 2 * HEAD_SIZE, HEAD_SIZE), HEAD_SIZE)]
                for h in range(2)
            ],
            axis=1,
        )

    def inside(slot):
        return lax.rem(slot, pair_slots) * rows

    def doubled(value):
        return jnp.concatenate(split(value), axis=0)

    def part_scores(slot):
        q = spread(q_all[slot], 2, pair_rows // 2, inside(slot))
        both = dot(doubled(dot(q, weight(slot, 0), NT)), x_v[...], NT)
        s_part[slot] = both[:rows] + both[rows:]

    def part_sums(slot):
        both = dot(doubled(dot(p_all[slot], x_v[...], NN)), weight(slot, 1), NN)
        o_part[slot] = gather_blocks(both[:rows] + both[rows:], 2, pair_rows // 2, inside(slot))

    for copy in w_copies:
        copy.wait()
    x_copy.wait()
    for peer in columns:
        part_scores(peer[1])
        deliver(s_part.at[peer[1]], s_land, peer, 1)
    part_scores(t)
    receive(s_land, columns, t_send.at[1], t_recv.at[1])

    scores = s_part[t]
    for _, i, _ in columns:
        scores = scores + s_land[i]
    scores = scores * scale
    top = jnp.max(scores, axis=1, keepdims=True)
    probs = jnp.exp(scores - top)
    p_all[t] = probs.astype(jnp.bfloat16)
    send(lambda i: p_all.at[t], p_all, t, columns, t_send.at[2], t_recv.at[2])
    marks[replica, 0] = jnp.broadcast_to(top, (rows, HEAD_SIZE))
    marks[replica, 1] = jnp.broadcast_to(jnp.sum(probs, axis=1, keepdims=True), (rows, HEAD_SIZE))
    send(lambda i: marks.at[replica], marks, replica, replicas, m_send, m_recv)

    part_sums(t)
    for peer in reversed(columns):
        receive(p_all, [peer], t_send.at[2], t_recv.at[2])
        part_sums(peer[1])
        deliver(o_part.at[peer[1]], o_land, peer, 3)

    receive(marks, replicas, m_send, m_recv)

    def prepare(k, carry):
        request = jnp.full((rows, HEAD_SIZE), replica * requests + k, jnp.int32)
        hits = [request == placement[i] for i in range(n_replica)]
        top = c_max[k]
        for i in range(n_replica):
            top = jnp.maximum(top, jnp.where(hits[i], marks[i, 0], HIDDEN))
        kept = jnp.exp(c_max[k] - top)
        total = c_sum[k] * kept
        added = []
        for i in range(n_replica):
            added.append(jnp.where(hits[i], jnp.exp(marks[i, 0] - top), 0.0))
            total = total + marks[i, 1] * added[i]
        inverse = 1.0 / total
        c_out[k] = c_out[k] * (kept * inverse)
        for i in range(n_replica):
            factors[k, i] = added[i] * inverse
        return carry

    lax.fori_loop(0, requests, prepare, 0)
    receive(o_land, columns, t_send.at[3], t_recv.at[3])
    summed = o_part[t]
    for _, i, _ in columns:
        summed = summed + o_land[i]
    state[replica] = summed

    send(lambda i: state.at[replica], state, replica, replicas, e_send, e_recv)
    receive(state, replicas, e_send, e_recv)

    def combine(k, carry):
        summed = c_out[k]
        for i in range(n_replica):
            summed = summed + state[i] * factors[k, i]
        c_out[k] = summed
        return carry

    lax.fori_loop(0, requests, combine, 0)
    for h in range(heads):
        out_ref[:, h * HEAD_SIZE:(h + 1) * HEAD_SIZE] = c_out[:, h, :].astype(out_ref.dtype)
    for copy in pending:
        copy.wait_send()


def local(sizes, span_hidden, key_value_weight, queries, kv_cache, block_table, lengths, placement):
    n_role, n_rep, n_tp = sizes
    n_replica = n_role * n_rep
    requests = queries.shape[0]
    heads = queries.shape[1] // HEAD_SIZE
    rows = max(heads, 16)
    tokens, features = span_hidden.shape
    pool = kv_cache.reshape(-1, PAGE_TOKENS, kv_cache.shape[1])
    bf16, f32 = jnp.bfloat16, jnp.float32
    smem = pl.BlockSpec(memory_space=pltpu.SMEM)
    vmem = pl.BlockSpec(memory_space=pltpu.VMEM)
    hbm = pl.BlockSpec(memory_space=pl.ANY)
    dma = pltpu.SemaphoreType.DMA
    return pl.pallas_call(
        functools.partial(kernel, sizes),
        out_shape=jax.ShapeDtypeStruct(queries.shape, bf16),
        in_specs=[smem, smem, smem, vmem, hbm, hbm, hbm],
        out_specs=vmem,
        scratch_shapes=[
            pltpu.VMEM(span_hidden.shape, bf16),
            pltpu.VMEM(key_value_weight.shape, bf16),
            pltpu.VMEM(pool.shape, bf16),
            pltpu.VMEM((requests, rows, HEAD_SIZE), f32),
            pltpu.VMEM((n_replica, rows, HEAD_SIZE), bf16),
            pltpu.VMEM((n_replica, rows, HEAD_SIZE), bf16),
            pltpu.VMEM((n_tp, rows, HEAD_SIZE), bf16),
            pltpu.VMEM((n_tp, rows, tokens), f32),
            pltpu.VMEM((n_tp, rows, tokens), f32),
            pltpu.VMEM((n_tp, rows, tokens), bf16),
            pltpu.VMEM((n_tp, rows, HEAD_SIZE), f32),
            pltpu.VMEM((n_tp, rows, HEAD_SIZE), f32),
            pltpu.VMEM((n_replica, rows, HEAD_SIZE), f32),
            pltpu.VMEM((n_replica, 2, rows, HEAD_SIZE), f32),
            pltpu.VMEM((requests, n_replica, rows, HEAD_SIZE), f32),
            pltpu.VMEM((requests, rows, HEAD_SIZE), f32),
            pltpu.VMEM((requests, rows, HEAD_SIZE), f32),
            pltpu.VMEM((requests, rows, HEAD_SIZE), f32),
            dma((3 + CHUNKS,)),
            dma((n_replica,)),
            dma((n_replica,)),
            dma((4, n_tp)),
            dma((4, n_tp)),
            dma((n_replica,)),
            dma((n_replica,)),
            dma((n_replica,)),
            dma((n_replica,)),
        ],
        compiler_params=pltpu.CompilerParams(
            collective_id=0, has_side_effects=True, vmem_limit_bytes=60 * 1024 * 1024
        ),
    )(placement, block_table.T, lengths, queries, span_hidden, key_value_weight, pool)


def solution(mesh):
    placed = (
        P(("role", "rep"), "tp"),
        P("tp", None),
        P(("role", "rep"), "tp"),
        P(("role", "rep"), "tp"),
        P(("role", "rep"), None),
        P(("role", "rep")),
        P(),
    )
    sizes = (mesh.shape["role"], mesh.shape["rep"], mesh.shape["tp"])
    return jax.shard_map(
        functools.partial(local, sizes),
        mesh=mesh, in_specs=placed, out_specs=P(("role", "rep"), "tp"), check_vma=False,
    )
```

```python
import functools

import jax
import jax.numpy as jnp
from jax import lax
from jax.experimental import pallas as pl
from jax.experimental.pallas import tpu as pltpu
from jax.sharding import PartitionSpec as P

HEAD_SIZE = 128
PAGE_TOKENS = 128
MESH = pl.DeviceIdType.MESH
HIDDEN = -1e30
CHUNKS = 4
NT = (((1,), (1,)), ((), ()))
NN = (((1,), (0,)), ((), ()))


def dot(a, b, dims):
    return lax.dot_general(a, b, dims, preferred_element_type=jnp.float32)


def split(value):
    high = value.astype(jnp.bfloat16)
    return high, (value - high.astype(jnp.float32)).astype(jnp.bfloat16)


def spread(rows, heads, each, first=0):
    if heads == 1:
        return rows
    owner = (lax.broadcasted_iota(jnp.int32, rows.shape, 0) + first) // each
    wide = rows.astype(jnp.float32)
    parts = [jnp.where(owner == h, wide, 0.0) for h in range(heads)]
    return jnp.concatenate(parts, axis=1).astype(jnp.bfloat16)


def gather_blocks(rows, heads, each, first=0):
    if heads == 1:
        return rows
    shape = (rows.shape[0], HEAD_SIZE)
    owner = (lax.broadcasted_iota(jnp.int32, shape, 0) + first) // each
    result = rows[:, :HEAD_SIZE]
    for h in range(1, heads):
        result = jnp.where(owner == h, rows[:, h * HEAD_SIZE:(h + 1) * HEAD_SIZE], result)
    return result


def kernel(
    sizes,
    placement, table, lengths, q_ref, x_hbm, w_hbm, cache_hbm,
    out_ref,
    x_v, w_v, cache_v, q_rows, chosen, q_land, q_all, s_part, s_land, p_all, p_hi, p_lo, o_part, o_land,
    state, marks, factors, c_out, c_max, c_sum,
    local_sem, a_send, a_recv, t_send, t_recv, m_send, m_recv, e_send, e_recv,
):
    n_role, n_rep, n_tp = sizes
    n_replica = n_role * n_rep
    scale = HEAD_SIZE ** -0.5
    requests, rows = q_rows.shape[0], q_rows.shape[1]
    heads = q_ref.shape[1] // HEAD_SIZE
    features = x_v.shape[1]
    local_heads = cache_v.shape[2] // (2 * HEAD_SIZE)
    pairs = w_v.shape[1] // (4 * HEAD_SIZE)
    pair_rows = n_tp * rows // pairs
    pair_slots = pair_rows // rows
    piece = features // CHUNKS
    slots = table.shape[0]

    replica = lax.axis_index("role") * n_rep + lax.axis_index("rep")
    t = lax.axis_index("tp")

    role, rep = lax.axis_index("role"), lax.axis_index("rep")

    def wrap(value, count):
        return jnp.where(value >= count, value - count, value)

    replicas = []
    for step in range(1, n_replica):
        to_role, to_rep = wrap(role + step // n_rep, n_role), wrap(rep + step % n_rep, n_rep)
        replicas.append((step, to_role * n_rep + to_rep, (to_role, to_rep, t)))
    columns = []
    for step in range(1, n_tp):
        down, up = n_tp - step, step - 1
        down = jnp.where(down <= t, down - 1, down)
        up = jnp.where(up >= t, up + 1, up)
        to_tp = jnp.where(2 * t < n_tp, down, up)
        columns.append((step, to_tp, (role, rep, to_tp)))

    barrier = pltpu.get_barrier_semaphore()
    for _, _, device in columns + replicas:
        pl.semaphore_signal(barrier, inc=1, device_id=device, device_id_type=MESH)
    half = cache_v.shape[0] // 2
    cache_copies = [
        pltpu.make_async_copy(
            cache_hbm.at[pl.ds(h * half, half)], cache_v.at[pl.ds(h * half, half)], local_sem.at[h]
        )
        for h in range(2)
    ]
    w_copies = [
        pltpu.make_async_copy(
            w_hbm.at[pl.ds(c * piece, piece)], w_v.at[pl.ds(c * piece, piece)], local_sem.at[2 + c]
        )
        for c in range(CHUNKS)
    ]
    x_copy = pltpu.make_async_copy(x_hbm, x_v, local_sem.at[2 + CHUNKS])
    for copy in cache_copies + w_copies + [x_copy]:
        copy.start()

    if rows > heads:
        q_rows[...] = jnp.zeros_like(q_rows)
    for h in range(heads):
        q_rows[:, h, :] = q_ref[:, h * HEAD_SIZE:(h + 1) * HEAD_SIZE].astype(jnp.float32)
    for i in range(n_replica):
        chosen[i] = q_rows[lax.rem(placement[i], requests)].astype(jnp.bfloat16)
    pl.semaphore_wait(barrier, n_replica + n_tp - 2)

    pending = []

    def send(source, land, slot, peers, send_sem, recv_sem):
        for d, i, device in peers:
            copy = pltpu.make_async_remote_copy(
                src_ref=source(i), dst_ref=land.at[slot],
                send_sem=send_sem.at[d], recv_sem=recv_sem.at[slot],
                device_id=device, device_id_type=MESH,
            )
            copy.start()
            pending.append(copy)

    def deliver(source, land, peer, part):
        d, i, device = peer
        copy = pltpu.make_async_remote_copy(
            src_ref=source, dst_ref=land.at[t],
            send_sem=t_send.at[part, d], recv_sem=t_recv.at[part, t],
            device_id=device, device_id_type=MESH,
        )
        copy.start()
        pending.append(copy)

    def receive(land, peers, send_sem, recv_sem):
        for d, i, device in peers:
            pltpu.make_async_remote_copy(
                src_ref=land.at[i], dst_ref=land.at[i],
                send_sem=send_sem.at[d], recv_sem=recv_sem.at[i],
                device_id=device, device_id_type=MESH,
            ).wait_recv()

    send(lambda i: chosen.at[i], q_land, replica, replicas, a_send, a_recv)
    q_land[replica] = chosen[replica]

    def cache_request(k):
        blocks = [
            cache_v[table[j, k]]
            for j in range(slots)
        ]
        block = jnp.concatenate(blocks, axis=0)

        def take(which):
            return jnp.concatenate(
                [
                    block[:, (2 * h + which) * HEAD_SIZE:(2 * h + which + 1) * HEAD_SIZE]
                    for h in range(local_heads)
                ],
                axis=1,
            )

        scores = dot(spread(q_rows[k].astype(jnp.bfloat16), local_heads, rows // local_heads), take(0), NT) * scale
        seen = lax.broadcasted_iota(jnp.int32, scores.shape, 1) < lengths[k]
        scores = jnp.where(seen, scores, HIDDEN)
        top = jnp.max(scores, axis=1, keepdims=True)
        probs = jnp.where(seen, jnp.exp(scores - top), 0.0)
        total = jnp.sum(probs, axis=1, keepdims=True)
        summed = dot(probs.astype(jnp.bfloat16), take(1), NN)
        c_out[k] = gather_blocks(summed, local_heads, rows // local_heads)
        c_max[k] = jnp.broadcast_to(top, (rows, HEAD_SIZE))
        c_sum[k] = jnp.broadcast_to(total, (rows, HEAD_SIZE))

    def cache_part(first, last):
        def body(step, carry):
            for u in range(2):
                cache_request(first + 2 * step + u)
            return carry

        lax.fori_loop(0, (last - first) // 2, body, 0)

    for copy in cache_copies:
        copy.wait()
    cache_part(0, requests // 2)

    receive(q_land, replicas, a_send, a_recv)
    q_all[t] = q_land[lax.div(placement[replica], requests)]
    send(lambda i: q_all.at[t], q_all, t, columns, t_send.at[0], t_recv.at[0])
    cache_part(requests // 2, 3 * requests // 4)
    receive(q_all, columns, t_send.at[0], t_recv.at[0])

    def weight(slot, which):
        left = (slot // pair_slots) * (4 * HEAD_SIZE) + which * HEAD_SIZE
        return jnp.concatenate(
            [
                w_v[:, pl.ds(pl.multiple_of(left + h * 2 * HEAD_SIZE, HEAD_SIZE), HEAD_SIZE)]
                for h in range(2)
            ],
            axis=1,
        )

    def inside(slot):
        return lax.rem(slot, pair_slots) * rows

    def doubled(value):
        return jnp.concatenate(split(value), axis=0)

    def part_scores(slot):
        q = spread(q_all[slot], 2, pair_rows // 2, inside(slot))
        both = dot(doubled(dot(q, weight(slot, 0), NT)), x_v[...], NT)
        s_part[slot] = both[:rows] + both[rows:]

    def part_sums(slot):
        both = dot(doubled(dot(p_all[slot], x_v[...], NN)), weight(slot, 1), NN)
        o_part[slot] = gather_blocks(both[:rows] + both[rows:], 2, pair_rows // 2, inside(slot))

    for copy in w_copies:
        copy.wait()
    x_copy.wait()
    for peer in columns:
        part_scores(peer[1])
        deliver(s_part.at[peer[1]], s_land, peer, 1)
    part_scores(t)
    cache_part(3 * requests // 4, requests)
    receive(s_land, columns, t_send.at[1], t_recv.at[1])

    scores = s_part[t]
    for _, i, _ in columns:
        scores = scores + s_land[i]
    scores = scores * scale
    top = jnp.max(scores, axis=1, keepdims=True)
    probs = jnp.exp(scores - top)
    p_all[t] = probs.astype(jnp.bfloat16)
    send(lambda i: p_all.at[t], p_all, t, columns, t_send.at[2], t_recv.at[2])
    marks[replica, 0] = jnp.broadcast_to(top, (rows, HEAD_SIZE))
    marks[replica, 1] = jnp.broadcast_to(jnp.sum(probs, axis=1, keepdims=True), (rows, HEAD_SIZE))
    send(lambda i: marks.at[replica], marks, replica, replicas, m_send, m_recv)

    receive(p_all, columns, t_send.at[2], t_recv.at[2])
    both = dot(p_all[...].reshape(n_tp * rows, p_all.shape[2]), x_v[...], NN)
    high, low = split(both)
    wide_hi = high.reshape(n_tp, rows, features)
    wide_lo = low.reshape(n_tp, rows, features)
    p_hi[...] = wide_hi
    p_lo[...] = wide_lo
    for peer in columns + [(0, t, None)]:
        slot = peer[1]
        both = dot(jnp.concatenate([p_hi[slot], p_lo[slot]], axis=0), weight(slot, 1), NN)
        o_part[slot] = gather_blocks(both[:rows] + both[rows:], 2, pair_rows // 2, inside(slot))
        if peer[2] is not None:
            deliver(o_part.at[slot], o_land, peer, 3)

    receive(marks, replicas, m_send, m_recv)

    def prepare(k, carry):
        request = jnp.full((rows, HEAD_SIZE), replica * requests + k, jnp.int32)
        hits = [request == placement[i] for i in range(n_replica)]
        top = c_max[k]
        for i in range(n_replica):
            top = jnp.maximum(top, jnp.where(hits[i], marks[i, 0], HIDDEN))
        kept = jnp.exp(c_max[k] - top)
        total = c_sum[k] * kept
        added = []
        for i in range(n_replica):
            added.append(jnp.where(hits[i], jnp.exp(marks[i, 0] - top), 0.0))
            total = total + marks[i, 1] * added[i]
        inverse = 1.0 / total
        c_out[k] = c_out[k] * (kept * inverse)
        for i in range(n_replica):
            factors[k, i] = added[i] * inverse
        return carry

    lax.fori_loop(0, requests // 2, prepare, 0)
    receive(o_land, columns, t_send.at[3], t_recv.at[3])
    summed = o_part[t]
    for _, i, _ in columns:
        summed = summed + o_land[i]
    state[replica] = summed

    send(lambda i: state.at[replica], state, replica, replicas, e_send, e_recv)
    lax.fori_loop(requests // 2, requests, prepare, 0)
    receive(state, replicas, e_send, e_recv)

    def combine(k, carry):
        summed = c_out[k]
        for i in range(n_replica):
            summed = summed + state[i] * factors[k, i]
        c_out[k] = summed
        return carry

    lax.fori_loop(0, requests, combine, 0)
    for h in range(heads):
        out_ref[:, h * HEAD_SIZE:(h + 1) * HEAD_SIZE] = c_out[:, h, :].astype(out_ref.dtype)
    for copy in pending:
        copy.wait_send()


def local(sizes, span_hidden, key_value_weight, queries, kv_cache, block_table, lengths, placement):
    n_role, n_rep, n_tp = sizes
    n_replica = n_role * n_rep
    requests = queries.shape[0]
    heads = queries.shape[1] // HEAD_SIZE
    rows = max(heads, 16)
    tokens, features = span_hidden.shape
    pool = kv_cache.reshape(-1, PAGE_TOKENS, kv_cache.shape[1])
    bf16, f32 = jnp.bfloat16, jnp.float32
    smem = pl.BlockSpec(memory_space=pltpu.SMEM)
    vmem = pl.BlockSpec(memory_space=pltpu.VMEM)
    hbm = pl.BlockSpec(memory_space=pl.ANY)
    dma = pltpu.SemaphoreType.DMA
    return pl.pallas_call(
        functools.partial(kernel, sizes),
        out_shape=jax.ShapeDtypeStruct(queries.shape, bf16),
        in_specs=[smem, smem, smem, vmem, hbm, hbm, hbm],
        out_specs=vmem,
        scratch_shapes=[
            pltpu.VMEM(span_hidden.shape, bf16),
            pltpu.VMEM(key_value_weight.shape, bf16),
            pltpu.VMEM(pool.shape, bf16),
            pltpu.VMEM((requests, rows, HEAD_SIZE), f32),
            pltpu.VMEM((n_replica, rows, HEAD_SIZE), bf16),
            pltpu.VMEM((n_replica, rows, HEAD_SIZE), bf16),
            pltpu.VMEM((n_tp, rows, HEAD_SIZE), bf16),
            pltpu.VMEM((n_tp, rows, tokens), f32),
            pltpu.VMEM((n_tp, rows, tokens), f32),
            pltpu.VMEM((n_tp, rows, tokens), bf16),
            pltpu.VMEM((n_tp, rows, features), bf16),
            pltpu.VMEM((n_tp, rows, features), bf16),
            pltpu.VMEM((n_tp, rows, HEAD_SIZE), f32),
            pltpu.VMEM((n_tp, rows, HEAD_SIZE), f32),
            pltpu.VMEM((n_replica, rows, HEAD_SIZE), f32),
            pltpu.VMEM((n_replica, 2, rows, HEAD_SIZE), f32),
            pltpu.VMEM((requests, n_replica, rows, HEAD_SIZE), f32),
            pltpu.VMEM((requests, rows, HEAD_SIZE), f32),
            pltpu.VMEM((requests, rows, HEAD_SIZE), f32),
            pltpu.VMEM((requests, rows, HEAD_SIZE), f32),
            dma((3 + CHUNKS,)),
            dma((n_replica,)),
            dma((n_replica,)),
            dma((4, n_tp)),
            dma((4, n_tp)),
            dma((n_replica,)),
            dma((n_replica,)),
            dma((n_replica,)),
            dma((n_replica,)),
        ],
        compiler_params=pltpu.CompilerParams(
            collective_id=0, has_side_effects=True, vmem_limit_bytes=60 * 1024 * 1024
        ),
    )(placement, block_table.T, lengths, queries, span_hidden, key_value_weight, pool)


def solution(mesh):
    placed = (
        P(("role", "rep"), "tp"),
        P("tp", None),
        P(("role", "rep"), "tp"),
        P(("role", "rep"), "tp"),
        P(("role", "rep"), None),
        P(("role", "rep")),
        P(),
    )
    sizes = (mesh.shape["role"], mesh.shape["rep"], mesh.shape["tp"])
    return jax.shard_map(
        functools.partial(local, sizes),
        mesh=mesh, in_specs=placed, out_specs=P(("role", "rep"), "tp"), check_vma=False,
    )
```
